32 devices in a mesh: frame: 8 (over z, y), chan: 4 (over x, core).
Axes of the slice: x: 2, y: 2, z: 4, core: 2. Of those that a mesh axis runs over, the one named last changes fastest.
Arguments:
- inputs: bfloat16 [1536, 3072], P('chan', 'frame'), may hold values from -6 to 6
- norm_gain: float32 [1536], replicated, may hold values from 0.5 to 2
- norm_bias: float32 [1536], replicated, may hold values from -3 to 3
- value_weight: bfloat16 [1536, 1536], P('chan'), may hold values from -0.15625 to 0.15625
- gate_weight: bfloat16 [1536, 1536], P('chan'), may hold values from -0.15625 to 0.15625
- conv_kernel: float32 [31, 1536], P(None, 'chan'), may hold values from -1 to 1
- project_weight: bfloat16 [1536, 1536], P('chan'), may hold values from -0.15625 to 0.15625
- frame_mask: int32 [3072], P('frame'), may hold values 0 or 1
- upstream: bfloat16 [1536, 3072], P('chan', 'frame'), may hold values from -6 to 6
Outputs:
- inputs_grad: bfloat16 [1536, 3072], P('chan', 'frame')
- value_grad: float32 [1536, 1536], P('chan', 'frame')
- gate_grad: float32 [1536, 1536], P('chan', 'frame')
- project_grad: float32 [1536, 1536], P('chan', 'frame')
- kernel_grad: float32 [31, 1536], P(None, 'chan')
- gain_grad: float32 [1536], P('chan')
- bias_grad: float32 [1536], P('chan')
The draws below stay inside these ranges and needn't reach their ends.
All inputs are finite; a program needn't handle non-finite values. No bound on the sum of `frame_mask` on one device may be relied on, other than what follows from the above.
Results may differ from the reference program's by a relative error of at most 0.025.
Values may be sent and summed in bfloat16 or wider, within the bound.
A program may use at most 64 MiB of HBM per device.

```python
import math
import jax
import jax.numpy as jnp
from jax import lax

D = 1536
KW = 31
FRAMES = 3072
N_CHAN = 4


def set_ends(entries, rng, low, high):
    longest = entries.shape.index(max(entries.shape))
    spots = []
    for shift in (0, 1):
        where = [jax.random.randint(jax.random.fold_in(rng, axis), (), 0, length) for axis, length in enumerate(entries.shape)]
        where[longest] = (where[longest] + shift) % entries.shape[longest]
        spots.append(tuple(where))
    return entries.at[spots[0]].set(low).at[spots[1]].set(high)


def with_spikes(values, own_key, source, target, blocks, factor):
    def block_of(axis_at):
        return (jnp.arange(values.shape[axis_at]) // (values.shape[axis_at] // blocks)).reshape((-1,) + (1,) * (values.ndim - 1 - axis_at))

    first = jax.random.permutation(own_key, blocks)[block_of(target)]
    far = (block_of(target) + blocks // 2) % blocks
    return jnp.where((block_of(source) == first) | (block_of(source) == far), factor * values, values)


def block_levels(key, extent, pieces, smallest, high):
    factor_of = 1.0
    for position, shards_of in pieces:
        heights = jax.random.uniform(jax.random.fold_in(jax.random.fold_in(key, 6), position), (shards_of,), jnp.float32, smallest / len(pieces), high / len(pieces))
        factor_of = factor_of * jnp.repeat(jnp.exp(heights), extent[position] // shards_of).reshape((-1,) + (1,) * (len(extent) - 1 - position))
    return factor_of


def normal_values(own_key, shape, width, most, pieces=(), dtype=jnp.bfloat16):
    values = jax.random.normal(own_key, shape, jnp.float32) * width
    if len(pieces) > 0:
        values = block_levels(own_key, shape, pieces, -0.22, 0.18) * values
    return jnp.clip(values, min=-most, max=most).astype(dtype)


def bell_draw_with(stream_key, shape, width, most, split, heavy, held_as=jnp.bfloat16):
    entries = width * jax.random.normal(stream_key, shape, jnp.float32)
    if split:
        entries = entries * block_levels(stream_key, shape, split, -0.22, 0.18)
    return jnp.clip(with_spikes(entries, jax.random.fold_in(stream_key, 3), *heavy), -most, most).astype(held_as)


def setup_inputs(seed: int = 0) -> dict:
    key_list = jax.random.split(jax.random.key(seed), 10)
    inputs = normal_values(key_list[0], (D, FRAMES), 1.0, 6.0, ((0, 4), (1, 8)))
    norm_gain = jnp.clip(jnp.exp(jax.random.uniform(key_list[1], (D,), jnp.float32, math.log(0.5), math.log(2.0))), 0.5, 2.0)
    norm_bias = normal_values(key_list[2], (D,), 0.5, 3.0, (), jnp.float32)
    value_weight = normal_values(key_list[3], (D, D), D ** -0.5, 0.15625, ((0, 4),))
    gate_weight = normal_values(key_list[4], (D, D), D ** -0.5, 0.15625, ((0, 4),))
    conv_kernel = normal_values(key_list[5], (KW, D), KW ** -0.5, 1.0, ((1, 4),), jnp.float32)
    project_weight = normal_values(key_list[6], (D, D), D ** -0.5, 0.15625, ((0, 4),))
    frame_mask = set_ends((jax.random.randint(key_list[7], (FRAMES,), 0, 8) < 7).astype(jnp.int32), jax.random.fold_in(key_list[7], 1), 0, 1)
    upstream = bell_draw_with(key_list[8], (D, FRAMES), 1.0, 6.0, ((0, 4), (1, 8)), (1, 0, 8, 2.0))
    return dict(inputs=inputs, norm_gain=norm_gain, norm_bias=norm_bias, value_weight=value_weight, gate_weight=gate_weight, conv_kernel=conv_kernel, project_weight=project_weight, frame_mask=frame_mask, upstream=upstream)


eps = 1e-05

def reference(inputs, norm_gain, norm_bias, value_weight, gate_weight, conv_kernel, project_weight, frame_mask, upstream):
    model_width = inputs.shape[0]
    frames = inputs.shape[1]
    taps = conv_kernel.shape[0]
    reach = taps // 2
    x_float = inputs.astype(jnp.float32)
    row_mean = lax.optimization_barrier(jnp.mean(x_float, axis=0, keepdims=True))
    row_var = lax.optimization_barrier(jnp.mean(x_float * x_float, axis=0, keepdims=True)) - row_mean * row_mean
    inv_std = lax.rsqrt(row_var + eps)
    centred = (x_float - row_mean) * inv_std
    normed = (centred * norm_gain[:, None] + norm_bias[:, None]).astype(jnp.bfloat16)
    value_proj = jnp.dot(value_weight, normed, preferred_element_type=jnp.float32)
    gate_proj = jnp.dot(gate_weight, normed, preferred_element_type=jnp.float32)
    gate_sig = jax.nn.sigmoid(gate_proj)
    keep = frame_mask.astype(jnp.float32)[None, :]
    glu_out = (value_proj * gate_sig * keep).astype(jnp.bfloat16)
    padded = jnp.pad(glu_out, ((0, 0), (reach, reach)))
    conv_out = jnp.zeros((model_width, frames), jnp.float32)
    for k in range(taps):
        conv_out = conv_out + conv_kernel[k][:, None] * padded[:, k:k + frames].astype(jnp.float32)
    conv_sig = jax.nn.sigmoid(conv_out)
    activated = (conv_out * conv_sig).astype(jnp.bfloat16)
    act_grad = jnp.dot(project_weight, upstream, preferred_element_type=jnp.float32).astype(jnp.bfloat16)
    project_grad = lax.dot_general(activated, upstream, (((1,), (1,)), ((), ())), preferred_element_type=jnp.float32)
    conv_grad = (act_grad.astype(jnp.float32) * (conv_sig + conv_out * conv_sig * (1.0 - conv_sig))).astype(jnp.bfloat16)
    back_pad = jnp.pad(conv_grad, ((0, 0), (reach, reach)))
    grad_float = conv_grad.astype(jnp.float32)
    glu_grad = jnp.zeros((model_width, frames), jnp.float32)
    kernel_rows = []
    for k in range(taps):
        glu_grad = glu_grad + conv_kernel[k][:, None] * back_pad[:, 2 * reach - k:2 * reach - k + frames].astype(jnp.float32)
        kernel_rows.append(lax.optimization_barrier(jnp.sum(grad_float * padded[:, k:k + frames].astype(jnp.float32), axis=1)))
    kernel_grad = jnp.stack(kernel_rows)
    glu_grad = glu_grad * keep
    value_back = (glu_grad * gate_sig).astype(jnp.bfloat16)
    gate_back = (glu_grad * value_proj * gate_sig * (1.0 - gate_sig)).astype(jnp.bfloat16)
    block = model_width // N_CHAN
    normed_grad = jnp.zeros((model_width, frames), jnp.float32)
    for j in range(N_CHAN):
        lower = j * block
        partial_term = lax.dot_general(value_weight[lower:lower + block], value_back[lower:lower + block], (((0,), (0,)), ((), ())), preferred_element_type=jnp.float32)
        partial_term = partial_term + lax.dot_general(gate_weight[lower:lower + block], gate_back[lower:lower + block], (((0,), (0,)), ((), ())), preferred_element_type=jnp.float32)
        rounded = lax.optimization_barrier(partial_term.astype(jnp.bfloat16))
        normed_grad = normed_grad + rounded.astype(jnp.float32)
    value_grad = lax.dot_general(value_back, normed, (((1,), (1,)), ((), ())), preferred_element_type=jnp.float32)
    gate_grad = lax.dot_general(gate_back, normed, (((1,), (1,)), ((), ())), preferred_element_type=jnp.float32)
    gain_grad = lax.optimization_barrier(jnp.sum(normed_grad * centred, axis=1))
    bias_grad = lax.optimization_barrier(jnp.sum(normed_grad, axis=1))
    scaled = normed_grad * norm_gain[:, None]
    first_sum = lax.optimization_barrier(jnp.sum(scaled, axis=0, keepdims=True)) / model_width
    second_sum = lax.optimization_barrier(jnp.sum(scaled * centred, axis=0, keepdims=True)) / model_width
    inputs_grad = (upstream.astype(jnp.float32) + inv_std * (scaled - first_sum - centred * second_sum)).astype(jnp.bfloat16)
    return (inputs_grad, value_grad, gate_grad, project_grad, kernel_grad, gain_grad, bias_grad)
```

```python
import functools

import jax
import jax.numpy as jnp
from jax import lax
from jax.experimental import pallas as pl
from jax.experimental.pallas import tpu as pltpu
from jax.sharding import PartitionSpec as P

eps = 1e-05
pad = 16
row_tile = 64
MESH = pl.DeviceIdType.MESH
f32 = jnp.float32
bf16 = jnp.bfloat16


def dot(a, b, dims):
    return lax.dot_general(a, b, (dims, ((), ())), preferred_element_type=f32)


NN = ((1,), (0,))
NT = ((1,), (1,))


def kernel(
    n, F, x_ref, u_ref, gain_ref, bias_ref, vw_ref, gw_ref, w_ref, pw_ref, keep_ref,
    dx_ref, vg_ref, gg_ref, pg_ref, kg_ref, gb_ref,
    full_x, full_u, normed, vwt, gwt, vp, gs, gl_pad, cg_pad, act_t, conv_t, kacc,
    halo, snd1, rcv1, own1, snd2, rcv2,
    csnd1, crcv1, cown, csnd2, crcv2, st_snd, st_rcv, gb_snd, gb_rcv,
    k_snd, k_rcv1, k_snd2, k_rcv2,
    sx, rx, su, ru, sh, rh, s1, r1, s2, r2, sc1, rc1, sc2, rc2, sst, rst, sgb, rgb,
    sk1, rk1, sk2, rk2,
):
    C, T = x_ref.shape
    D = vw_ref.shape[1]
    taps = w_ref.shape[0]
    G = F // 2
    M = n // 2
    W = D // F
    me = lax.axis_index("chan")
    fr = lax.axis_index("frame")
    core = lax.rem(me, 2)
    chip = me // 2
    sib = me + 1 - 2 * core
    par = lax.rem(fr, 2)
    grp = fr // 2
    pair = fr + 1 - 2 * par
    pending = []

    def copy(src, dst, ssem, rsem, axis, index):
        return pltpu.make_async_remote_copy(
            src_ref=src, dst_ref=dst, send_sem=ssem, recv_sem=rsem,
            device_id={axis: index}, device_id_type=MESH,
        )

    def send(*args):
        c = copy(*args)
        c.start()
        pending.append(c)

    def rows(i, size):
        return pl.ds(pl.multiple_of(i * size, 16), size)

    barrier = pltpu.get_barrier_semaphore()
    for j in range(1, n):
        pl.semaphore_signal(
            barrier, inc=1, device_id={"chan": lax.rem(me + j, n)}, device_id_type=MESH
        )
    for j in range(1, F):
        pl.semaphore_signal(
            barrier, inc=1, device_id={"frame": lax.rem(fr + j, F)}, device_id_type=MESH
        )
    pl.semaphore_wait(barrier, n - 1 + F - 1)

    for ref, full, ss, rs in ((x_ref, full_x, sx, rx), (u_ref, full_u, su, ru)):
        for j in range(1, M):
            send(ref, full.at[rows(me, C)], ss.at[j], rs.at[me], "chan", lax.rem(me + 2 * j, n))
        send(ref, full.at[rows(me, C)], ss.at[0], rs.at[me], "chan", sib)
    full_x[rows(me, C), :] = x_ref[...]
    full_u[rows(me, C), :] = u_ref[...]
    vwt[...] = vw_ref[...].T
    gwt[...] = gw_ref[...].T

    def arrive(full, ss, rs, src):
        slot = full.at[rows(src, C)]
        copy(slot, slot, ss, rs.at[src], "chan", sib).wait_recv()

    def forward(full, ss, rs):
        for j in range(1, M):
            src = lax.rem(me + 2 * j, n)
            arrive(full, ss.at[0], rs, src)
            slot = full.at[rows(src, C)]
            send(slot, slot, ss.at[M + j - 1], rs.at[src], "chan", sib)

    def rest(full, ss, rs):
        for j in range(M):
            arrive(full, ss.at[0], rs, lax.rem(sib + 2 * j, n))

    forward(full_x, sx, rx)
    rest(full_x, sx, rx)
    total = jnp.zeros((1, T), f32)
    square = jnp.zeros((1, T), f32)
    for j in range(n):
        x = full_x[j * C : (j + 1) * C, :].astype(f32)
        total = total + jnp.sum(x, axis=0, keepdims=True)
        square = square + jnp.sum(x * x, axis=0, keepdims=True)
    mean = total / D
    inv_std = lax.rsqrt(square / D - mean * mean + eps)
    for j in range(n):
        x = full_x[j * C : (j + 1) * C, :].astype(f32)
        normed[j * C : (j + 1) * C, :] = (
            (x - mean) * inv_std * gain_ref[j] + bias_ref[j]
        ).astype(bf16)
    keep = keep_ref[...]
    vp[...] = dot(vw_ref[...], normed[...], NN)
    gs[...] = jax.nn.sigmoid(dot(gw_ref[...], normed[...], NN))
    glu = (vp[...] * gs[...] * keep).astype(bf16).astype(f32)
    gl_pad[0, pad : pad + T, :] = glu.T

    def edges(ref, which):
        right, left = lax.rem(fr + 1, F), lax.rem(fr + F - 1, F)
        a, b = 2 * which, 2 * which + 1
        send(ref.at[0, T : T + pad], halo.at[a], sh.at[a], rh.at[a], "frame", right)
        send(ref.at[0, pad : 2 * pad], halo.at[b], sh.at[b], rh.at[b], "frame", left)

    def edges_done(ref, which):
        a, b = 2 * which, 2 * which + 1
        copy(halo.at[a], halo.at[a], sh.at[a], rh.at[a], "frame", pair).wait_recv()
        copy(halo.at[b], halo.at[b], sh.at[b], rh.at[b], "frame", pair).wait_recv()
        ref[0, 0:pad, :] = jnp.where(fr > 0, halo[a], 0.0)
        ref[0, pad + T : T + 2 * pad, :] = jnp.where(fr < F - 1, halo[b], 0.0)
        span = T + 2 * pad - 8
        for p in range(1, 8):
            ref[p, 0:span, :] = ref[0, p : p + span, :]

    edges(gl_pad, 0)
    forward(full_u, su, ru)
    rest(full_u, su, ru)
    act_t[...] = dot(pw_ref[...], full_u[...], NN).astype(bf16).astype(f32).T
    edges_done(gl_pad, 0)

    lane_tile = 128 if C % 128 == 0 else C
    reach = taps // 2
    shift = pad - reach

    def window(ref, start, offset, lanes):
        return ref[offset % 8, pl.ds(start + offset // 8 * 8, row_tile), lanes]

    def conv_rows(i, carry):
        start = pl.multiple_of(i * row_tile, row_tile)
        for c0 in range(0, C, lane_tile):
            lanes = slice(c0, c0 + lane_tile)
            acc = jnp.zeros((row_tile, lane_tile), f32)
            for k in range(taps):
                acc = acc + w_ref[k : k + 1, lanes] * window(gl_pad, start, k + shift, lanes)
            s = jax.nn.sigmoid(acc)
            conv_t[pl.ds(start, row_tile), lanes] = (acc * s).astype(bf16)
            grad = act_t[pl.ds(start, row_tile), lanes] * (s + acc * s * (1.0 - s))
            cg_pad[0, pl.ds(start + pad, row_tile), lanes] = grad.astype(bf16).astype(f32)
        return carry

    lax.fori_loop(0, T // row_tile, conv_rows, 0)
    edges(cg_pad, 1)

    def part(arr, grad_of, fulls):
        for m in range(G):
            snd1[arr, m] = grad_of(fulls[rows(2 * m + 1 - par, W), :]).astype(bf16)
        send(snd1.at[arr], rcv1.at[arr], s1.at[arr], r1.at[arr], "frame", pair)

    def own_part(arr, grad_of, fulls):
        for m in range(G):
            own1[arr, m] = grad_of(fulls[rows(2 * m + par, W), :])

    def project_of(block):
        return dot(block, conv_t[...], NN)

    part(0, project_of, full_u)
    edges_done(cg_pad, 1)
    kacc[...] = jnp.zeros_like(kacc)

    def back_rows(i, carry):
        start = pl.multiple_of(i * row_tile, row_tile)
        for c0 in range(0, C, lane_tile):
            lanes = slice(c0, c0 + lane_tile)
            acc = jnp.zeros((row_tile, lane_tile), f32)
            here = window(cg_pad, start, pad, lanes)
            for k in range(taps):
                acc = acc + w_ref[k : k + 1, lanes] * window(cg_pad, start, pad + reach - k, lanes)
                prod = here * window(gl_pad, start, k + shift, lanes)
                kacc[8 * k : 8 * k + 8, lanes] += jnp.sum(
                    prod.reshape(row_tile // 8, 8, lane_tile), axis=0
                )
            act_t[pl.ds(start, row_tile), lanes] = acc
        return carry

    lax.fori_loop(0, T // row_tile, back_rows, 0)
    glu_grad = act_t[...].T * keep * gs[...]
    value_back = glu_grad.astype(bf16)
    gate_back = (glu_grad * vp[...] * (1.0 - gs[...])).astype(bf16)

    def value_of(block):
        return dot(block, value_back, NT)

    def gate_of(block):
        return dot(block, gate_back, NT)

    part(1, value_of, normed)

    def partial_term(j):
        return (
            dot(vwt[rows(j, C), :], value_back, NN) + dot(gwt[rows(j, C), :], gate_back, NN)
        ).astype(bf16)

    for m in range(M):
        csnd1[m] = partial_term(2 * m + 1 - core)
    send(csnd1, crcv1, sc1, rc1, "chan", sib)
    part(2, gate_of, normed)
    k_snd[...] = jnp.sum(kacc[...].reshape(kacc.shape[0] // 8, 8, C), axis=1)
    send(k_snd, k_rcv1, sk1, rk1, "frame", pair)
    for m in range(M):
        cown[m] = partial_term(2 * m + core)

    def second(arr):
        copy(snd1.at[arr], rcv1.at[arr], s1.at[arr], r1.at[arr], "frame", pair).wait_recv()
        for j in range(1, G):
            other = lax.rem(grp + j, G)
            snd2[arr, j] = (own1[arr, other] + rcv1[arr, other].astype(f32)).astype(bf16)
            send(
                snd2.at[arr, j], rcv2.at[arr, j], s2.at[arr, j], r2.at[arr, j],
                "frame", 2 * other + par,
            )

    own_part(0, project_of, full_u)
    second(0)

    copy(csnd1, crcv1, sc1, rc1, "chan", sib).wait_recv()
    for j in range(1, M):
        other = lax.rem(chip + j, M)
        csnd2[j] = (cown[other].astype(f32) + crcv1[other].astype(f32)).astype(bf16)
        send(
            csnd2.at[j], crcv2.at[j], sc2.at[j], rc2.at[j], "chan", 2 * other + core
        )
    own_part(1, value_of, normed)
    own_part(2, gate_of, normed)
    second(1)

    grad = cown[chip].astype(f32) + crcv1[chip].astype(f32)
    for j in range(1, M):
        copy(csnd2.at[j], crcv2.at[j], sc2.at[j], rc2.at[j], "chan", sib).wait_recv()
        grad = grad + crcv2[j].astype(f32)
    vp[...] = grad
    centred = (x_ref[...].astype(f32) - mean) * inv_std
    scaled = grad * gain_ref[me]
    st_snd[0:1, :] = jnp.sum(scaled, axis=0, keepdims=True)
    st_snd[1:2, :] = jnp.sum(scaled * centred, axis=0, keepdims=True)
    st_snd[2:8, :] = jnp.zeros((6, T), f32)
    for j in range(1, n):
        send(st_snd, st_rcv.at[j], sst.at[j], rst.at[j], "chan", lax.rem(me + j, n))
    gain_col = jnp.sum(grad * centred, axis=1, keepdims=True)
    bias_col = jnp.sum(grad, axis=1, keepdims=True)
    lane = lax.broadcasted_iota(jnp.int32, (C, 128), 1)
    gb_snd[...] = jnp.where(lane == 0, gain_col, bias_col).T[0:8, :]
    for j in range(1, F):
        send(gb_snd, gb_rcv.at[j], sgb.at[j], rgb.at[j], "frame", lax.rem(fr + j, F))

    copy(k_snd, k_rcv1, sk1, rk1, "frame", pair).wait_recv()
    k_snd2[...] = k_snd[...] + k_rcv1[...]
    for j in range(1, G):
        send(
            k_snd2, k_rcv2.at[j], sk2.at[j], rk2.at[j], "frame",
            2 * lax.rem(grp + j, G) + par,
        )
    second(2)

    stats = st_snd[...]
    for j in range(1, n):
        copy(st_snd, st_rcv.at[j], sst.at[j], rst.at[j], "chan", sib).wait_recv()
        stats = stats + st_rcv[j]
    stats = stats / D
    centred = (x_ref[...].astype(f32) - mean) * inv_std
    dx_ref[...] = (
        u_ref[...].astype(f32)
        + inv_std * (vp[...] * gain_ref[me] - stats[0:1, :] - centred * stats[1:2, :])
    ).astype(bf16)

    both = gb_snd[...]
    for j in range(1, F):
        copy(gb_snd, gb_rcv.at[j], sgb.at[j], rgb.at[j], "frame", pair).wait_recv()
        both = both + gb_rcv[j]
    gb_ref[...] = both
    taps_sum = k_snd2[...]
    for j in range(1, G):
        copy(k_snd2, k_rcv2.at[j], sk2.at[j], rk2.at[j], "frame", pair).wait_recv()
        taps_sum = taps_sum + k_rcv2[j]
    kg_ref[...] = taps_sum[0:taps, :]

    for arr, out in ((0, pg_ref), (1, vg_ref), (2, gg_ref)):
        acc = own1[arr, grp] + rcv1[arr, grp].astype(f32)
        for j in range(1, G):
            copy(
                snd2.at[arr, j], rcv2.at[arr, j], s2.at[arr, j], r2.at[arr, j], "frame", pair
            ).wait_recv()
            acc = acc + rcv2[arr, j].astype(f32)
        out[...] = acc.T

    for c in pending:
        c.wait_send()


def on_device(
    n, F, inputs, norm_gain, norm_bias, value_weight, gate_weight, conv_kernel,
    project_weight, frame_mask, upstream,
):
    C, T = inputs.shape
    D = value_weight.shape[1]
    taps = conv_kernel.shape[0]
    krows = -(-taps // 8) * 8
    G, M, W = F // 2, n // 2, D // F
    V = pltpu.VMEM
    S = pltpu.SemaphoreType.DMA
    scratch = [
        V((D, T), bf16), V((D, T), bf16), V((D, T), bf16), V((D, C), bf16), V((D, C), bf16),
        V((C, T), f32), V((C, T), f32), V((8, T + 2 * pad, C), f32), V((8, T + 2 * pad, C), f32),
        V((T, C), f32), V((T, C), bf16), V((8 * krows, C), f32),
        V((4, pad, C), f32),
        V((3, G, W, C), bf16), V((3, G, W, C), bf16), V((3, G, W, C), f32),
        V((3, G, W, C), bf16), V((3, G, W, C), bf16),
        V((M, C, T), bf16), V((M, C, T), bf16), V((M, C, T), bf16),
        V((M, C, T), bf16), V((M, C, T), bf16),
        V((8, T), f32), V((n, 8, T), f32), V((8, C), f32), V((F, 8, C), f32),
        V((krows, C), f32), V((krows, C), f32), V((krows, C), f32), V((G, krows, C), f32),
        S((n,)), S((n,)), S((n,)), S((n,)), S((4,)), S((4,)),
        S((3,)), S((3,)), S((3, G)), S((3, G)),
        S(()), S(()), S((M,)), S((M,)), S((n,)), S((n,)), S((F,)), S((F,)),
        S(()), S(()), S((G,)), S((G,)),
    ]
    out = jax.ShapeDtypeStruct
    vmem = pl.BlockSpec(memory_space=pltpu.VMEM)
    dx, vg, gg, pg, kg, gb = pl.pallas_call(
        functools.partial(kernel, n, F),
        out_shape=[
            out((C, T), bf16), out((C, W), f32), out((C, W), f32), out((C, W), f32),
            out((taps, C), f32), out((8, C), f32),
        ],
        in_specs=[vmem] * 9,
        out_specs=[vmem] * 6,
        scratch_shapes=scratch,
        compiler_params=pltpu.CompilerParams(
            collective_id=0, has_side_effects=True, vmem_limit_bytes=60 * 1024 * 1024
        ),
    )(
        inputs, upstream, norm_gain.reshape(n, C, 1), norm_bias.reshape(n, C, 1),
        value_weight, gate_weight, conv_kernel, project_weight,
        frame_mask.astype(f32)[None, :],
    )
    return dx, vg, gg, pg, kg, gb[0], gb[1]


def solution(mesh):
    return jax.shard_map(
        functools.partial(on_device, mesh.shape["chan"], mesh.shape["frame"]),
        mesh=mesh,
        in_specs=(
            P("chan", "frame"),
            P(),
            P(),
            P("chan", None),
            P("chan", None),
            P(None, "chan"),
            P("chan", None),
            P("frame"),
            P("chan", "frame"),
        ),
        out_specs=(
            P("chan", "frame"),
            P("chan", "frame"),
            P("chan", "frame"),
            P("chan", "frame"),
            P(None, "chan"),
            P("chan"),
            P("chan"),
        ),
        check_vma=False,
    )
```

```python
import functools

import jax
import jax.numpy as jnp
from jax import lax
from jax.experimental import pallas as pl
from jax.experimental.pallas import tpu as pltpu
from jax.sharding import PartitionSpec as P

eps = 1e-05
pad = 16
row_tile = 64
MESH = pl.DeviceIdType.MESH
f32 = jnp.float32
bf16 = jnp.bfloat16


def dot(a, b, dims):
    return lax.dot_general(a, b, (dims, ((), ())), preferred_element_type=f32)


NN = ((1,), (0,))
NT = ((1,), (1,))


def kernel(
    n, F, x_ref, u_ref, gain_ref, bias_ref, vw_ref, gw_ref, w_ref, pw_ref, keep_ref,
    dx_ref, vg_ref, gg_ref, pg_ref, kg_ref, gb_ref,
    full_x, full_u, normed, vwt, gwt, vp, gs, gl_pad, cg_pad, act_t, conv_t, kacc,
    halo, snd1, rcv1, own1, snd2, rcv2,
    csnd1, crcv1, cown, csnd2, crcv2, st_snd, st_rcv, gb_snd, gb_rcv,
    k_snd, k_rcv1, k_snd2, k_rcv2,
    gain_at, bias_at, sx, rx, su, ru, sh, rh, s1, r1, s2, r2, sc1, rc1, sc2, rc2, sst, rst, sgb, rgb,
    sk1, rk1, sk2, rk2,
):
    C, T = x_ref.shape
    D = vw_ref.shape[1]
    taps = w_ref.shape[0]
    G = F // 2
    M = n // 2
    W = D // F
    me = lax.axis_index("chan")
    fr = lax.axis_index("frame")
    core = lax.rem(me, 2)
    chip = me // 2
    sib = me + 1 - 2 * core
    par = lax.rem(fr, 2)
    grp = fr // 2
    pair = fr + 1 - 2 * par
    pending = []

    def copy(src, dst, ssem, rsem, axis, index):
        return pltpu.make_async_remote_copy(
            src_ref=src, dst_ref=dst, send_sem=ssem, recv_sem=rsem,
            device_id={axis: index}, device_id_type=MESH,
        )

    def send(*args):
        c = copy(*args)
        c.start()
        pending.append(c)

    def rows(i, size):
        return pl.ds(pl.multiple_of(i * size, 16), size)

    barrier = pltpu.get_barrier_semaphore()
    for j in range(1, n):
        pl.semaphore_signal(
            barrier, inc=1, device_id={"chan": lax.rem(me + j, n)}, device_id_type=MESH
        )
    for j in range(1, F):
        pl.semaphore_signal(
            barrier, inc=1, device_id={"frame": lax.rem(fr + j, F)}, device_id_type=MESH
        )
    pl.semaphore_wait(barrier, n - 1 + F - 1)

    for ref, full, ss, rs in ((x_ref, full_x, sx, rx), (u_ref, full_u, su, ru)):
        for j in range(1, M):
            send(ref, full.at[rows(me, C)], ss.at[j], rs.at[me], "chan", lax.rem(me + 2 * j, n))
        send(ref, full.at[rows(me, C)], ss.at[0], rs.at[me], "chan", sib)
    full_x[rows(me, C), :] = x_ref[...]
    full_u[rows(me, C), :] = u_ref[...]
    gain_at[...] = jnp.broadcast_to(gain_ref[...], (128, D)).T
    bias_at[...] = jnp.broadcast_to(bias_ref[...], (128, D)).T
    vwt[...] = vw_ref[...].T
    gwt[...] = gw_ref[...].T

    def arrive(full, ss, rs, src):
        slot = full.at[rows(src, C)]
        copy(slot, slot, ss, rs.at[src], "chan", sib).wait_recv()

    def forward(full, ss, rs):
        for j in range(1, M):
            src = lax.rem(me + 2 * j, n)
            arrive(full, ss.at[0], rs, src)
            slot = full.at[rows(src, C)]
            send(slot, slot, ss.at[M + j - 1], rs.at[src], "chan", sib)

    def rest(full, ss, rs):
        for j in range(M):
            arrive(full, ss.at[0], rs, lax.rem(sib + 2 * j, n))

    forward(full_x, sx, rx)
    rest(full_x, sx, rx)
    total = jnp.zeros((1, T), f32)
    square = jnp.zeros((1, T), f32)
    for j in range(n):
        x = full_x[j * C : (j + 1) * C, :].astype(f32)
        total = total + jnp.sum(x, axis=0, keepdims=True)
        square = square + jnp.sum(x * x, axis=0, keepdims=True)
    mean = total / D
    inv_std = lax.rsqrt(square / D - mean * mean + eps)
    for j in range(n):
        x = full_x[j * C : (j + 1) * C, :].astype(f32)
        normed[j * C : (j + 1) * C, :] = (
            (x - mean) * inv_std * gain_at[j * C : (j + 1) * C, 0:1]
            + bias_at[j * C : (j + 1) * C, 0:1]
        ).astype(bf16)
    keep = keep_ref[...]
    vp[...] = dot(vw_ref[...], normed[...], NN)
    gs[...] = jax.nn.sigmoid(dot(gw_ref[...], normed[...], NN))
    glu = (vp[...] * gs[...] * keep).astype(bf16).astype(f32)
    gl_pad[0, pad : pad + T, :] = glu.T

    def edges(ref, which):
        right, left = lax.rem(fr + 1, F), lax.rem(fr + F - 1, F)
        a, b = 2 * which, 2 * which + 1
        send(ref.at[0, T : T + pad], halo.at[a], sh.at[a], rh.at[a], "frame", right)
        send(ref.at[0, pad : 2 * pad], halo.at[b], sh.at[b], rh.at[b], "frame", left)

    def edges_done(ref, which):
        a, b = 2 * which, 2 * which + 1
        copy(halo.at[a], halo.at[a], sh.at[a], rh.at[a], "frame", pair).wait_recv()
        copy(halo.at[b], halo.at[b], sh.at[b], rh.at[b], "frame", pair).wait_recv()
        ref[0, 0:pad, :] = jnp.where(fr > 0, halo[a], 0.0)
        ref[0, pad + T : T + 2 * pad, :] = jnp.where(fr < F - 1, halo[b], 0.0)
        span = T + 2 * pad - 8
        for p in range(1, 8):
            ref[p, 0:span, :] = ref[0, p : p + span, :]

    edges(gl_pad, 0)
    forward(full_u, su, ru)
    rest(full_u, su, ru)
    act_t[...] = dot(pw_ref[...], full_u[...], NN).astype(bf16).astype(f32).T
    edges_done(gl_pad, 0)

    lane_tile = 128 if C % 128 == 0 else C
    reach = taps // 2
    shift = pad - reach

    def window(ref, start, offset, lanes):
        return ref[offset % 8, pl.ds(start + offset // 8 * 8, row_tile), lanes]

    def conv_rows(i, carry):
        start = pl.multiple_of(i * row_tile, row_tile)
        for c0 in range(0, C, lane_tile):
            lanes = slice(c0, c0 + lane_tile)
            acc = jnp.zeros((row_tile, lane_tile), f32)
            for k in range(taps):
                acc = acc + w_ref[k : k + 1, lanes] * window(gl_pad, start, k + shift, lanes)
            s = jax.nn.sigmoid(acc)
            conv_t[pl.ds(start, row_tile), lanes] = (acc * s).astype(bf16)
            grad = act_t[pl.ds(start, row_tile), lanes] * (s + acc * s * (1.0 - s))
            cg_pad[0, pl.ds(start + pad, row_tile), lanes] = grad.astype(bf16).astype(f32)
        return carry

    lax.fori_loop(0, T // row_tile, conv_rows, 0)
    edges(cg_pad, 1)

    def part(arr, grad_of, fulls):
        for m in range(G):
            snd1[arr, m] = grad_of(fulls[rows(2 * m + 1 - par, W), :]).astype(bf16)
        send(snd1.at[arr], rcv1.at[arr], s1.at[arr], r1.at[arr], "frame", pair)

    def own_part(arr, grad_of, fulls):
        for m in range(G):
            own1[arr, m] = grad_of(fulls[rows(2 * m + par, W), :])

    def project_of(block):
        return dot(block, conv_t[...], NN)

    part(0, project_of, full_u)
    edges_done(cg_pad, 1)
    kacc[...] = jnp.zeros_like(kacc)

    def back_rows(i, carry):
        start = pl.multiple_of(i * row_tile, row_tile)
        for c0 in range(0, C, lane_tile):
            lanes = slice(c0, c0 + lane_tile)
            acc = jnp.zeros((row_tile, lane_tile), f32)
            here = window(cg_pad, start, pad, lanes)
            for k in range(taps):
                acc = acc + w_ref[k : k + 1, lanes] * window(cg_pad, start, pad + reach - k, lanes)
                prod = here * window(gl_pad, start, k + shift, lanes)
                kacc[8 * k : 8 * k + 8, lanes] += jnp.sum(
                    prod.reshape(row_tile // 8, 8, lane_tile), axis=0
                )
            act_t[pl.ds(start, row_tile), lanes] = acc
        return carry

    lax.fori_loop(0, T // row_tile, back_rows, 0)
    glu_grad = act_t[...].T * keep * gs[...]
    value_back = glu_grad.astype(bf16)
    gate_back = (glu_grad * vp[...] * (1.0 - gs[...])).astype(bf16)

    def value_of(block):
        return dot(block, value_back, NT)

    def gate_of(block):
        return dot(block, gate_back, NT)

    part(1, value_of, normed)

    def partial_term(j):
        return (
            dot(vwt[rows(j, C), :], value_back, NN) + dot(gwt[rows(j, C), :], gate_back, NN)
        ).astype(bf16)

    for m in range(M):
        csnd1[m] = partial_term(2 * m + 1 - core)
    send(csnd1, crcv1, sc1, rc1, "chan", sib)
    part(2, gate_of, normed)
    k_snd[...] = jnp.sum(kacc[...].reshape(kacc.shape[0] // 8, 8, C), axis=1)
    send(k_snd, k_rcv1, sk1, rk1, "frame", pair)
    for m in range(M):
        cown[m] = partial_term(2 * m + core)

    def second(arr):
        copy(snd1.at[arr], rcv1.at[arr], s1.at[arr], r1.at[arr], "frame", pair).wait_recv()
        for j in range(1, G):
            other = lax.rem(grp + j, G)
            snd2[arr, j] = (own1[arr, other] + rcv1[arr, other].astype(f32)).astype(bf16)
            send(
                snd2.at[arr, j], rcv2.at[arr, j], s2.at[arr, j], r2.at[arr, j],
                "frame", 2 * other + par,
            )

    own_part(0, project_of, full_u)
    second(0)

    copy(csnd1, crcv1, sc1, rc1, "chan", sib).wait_recv()
    for j in range(1, M):
        other = lax.rem(chip + j, M)
        csnd2[j] = (cown[other].astype(f32) + crcv1[other].astype(f32)).astype(bf16)
        send(
            csnd2.at[j], crcv2.at[j], sc2.at[j], rc2.at[j], "chan", 2 * other + core
        )
    own_part(1, value_of, normed)
    own_part(2, gate_of, normed)
    second(1)

    grad = cown[chip].astype(f32) + crcv1[chip].astype(f32)
    for j in range(1, M):
        copy(csnd2.at[j], crcv2.at[j], sc2.at[j], rc2.at[j], "chan", sib).wait_recv()
        grad = grad + crcv2[j].astype(f32)
    vp[...] = grad
    centred = (x_ref[...].astype(f32) - mean) * inv_std
    scaled = grad * gain_at[rows(me, C), 0:1]
    st_snd[0:1, :] = jnp.sum(scaled, axis=0, keepdims=True)
    st_snd[1:2, :] = jnp.sum(scaled * centred, axis=0, keepdims=True)
    st_snd[2:8, :] = jnp.zeros((6, T), f32)
    for j in range(1, n):
        send(st_snd, st_rcv.at[j], sst.at[j], rst.at[j], "chan", lax.rem(me + j, n))
    gain_col = jnp.sum(grad * centred, axis=1, keepdims=True)
    bias_col = jnp.sum(grad, axis=1, keepdims=True)
    lane = lax.broadcasted_iota(jnp.int32, (C, 128), 1)
    gb_snd[...] = jnp.where(lane == 0, gain_col, bias_col).T[0:8, :]
    for j in range(1, F):
        send(gb_snd, gb_rcv.at[j], sgb.at[j], rgb.at[j], "frame", lax.rem(fr + j, F))

    copy(k_snd, k_rcv1, sk1, rk1, "frame", pair).wait_recv()
    k_snd2[...] = k_snd[...] + k_rcv1[...]
    for j in range(1, G):
        send(
            k_snd2, k_rcv2.at[j], sk2.at[j], rk2.at[j], "frame",
            2 * lax.rem(grp + j, G) + par,
        )
    second(2)

    stats = st_snd[...]
    for j in range(1, n):
        copy(st_snd, st_rcv.at[j], sst.at[j], rst.at[j], "chan", sib).wait_recv()
        stats = stats + st_rcv[j]
    stats = stats / D
    centred = (x_ref[...].astype(f32) - mean) * inv_std
    dx_ref[...] = (
        u_ref[...].astype(f32)
        + inv_std * (vp[...] * gain_at[rows(me, C), 0:1] - stats[0:1, :] - centred * stats[1:2, :])
    ).astype(bf16)

    both = gb_snd[...]
    for j in range(1, F):
        copy(gb_snd, gb_rcv.at[j], sgb.at[j], rgb.at[j], "frame", pair).wait_recv()
        both = both + gb_rcv[j]
    gb_ref[...] = both
    taps_sum = k_snd2[...]
    for j in range(1, G):
        copy(k_snd2, k_rcv2.at[j], sk2.at[j], rk2.at[j], "frame", pair).wait_recv()
        taps_sum = taps_sum + k_rcv2[j]
    kg_ref[...] = taps_sum[0:taps, :]

    for arr, out in ((0, pg_ref), (1, vg_ref), (2, gg_ref)):
        acc = own1[arr, grp] + rcv1[arr, grp].astype(f32)
        for j in range(1, G):
            copy(
                snd2.at[arr, j], rcv2.at[arr, j], s2.at[arr, j], r2.at[arr, j], "frame", pair
            ).wait_recv()
            acc = acc + rcv2[arr, j].astype(f32)
        out[...] = acc

    for c in pending:
        c.wait_send()


def on_device(
    n, F, inputs, norm_gain, norm_bias, value_weight, gate_weight, conv_kernel,
    project_weight, frame_mask, upstream,
):
    C, T = inputs.shape
    D = value_weight.shape[1]
    taps = conv_kernel.shape[0]
    krows = -(-taps // 8) * 8
    G, M, W = F // 2, n // 2, D // F
    V = pltpu.VMEM
    S = pltpu.SemaphoreType.DMA
    scratch = [
        V((D, T), bf16), V((D, T), bf16), V((D, T), bf16), V((D, C), bf16), V((D, C), bf16),
        V((C, T), f32), V((C, T), f32), V((8, T + 2 * pad, C), f32), V((8, T + 2 * pad, C), f32),
        V((T, C), f32), V((T, C), bf16), V((8 * krows, C), f32),
        V((4, pad, C), f32),
        V((3, G, W, C), bf16), V((3, G, W, C), bf16), V((3, G, W, C), f32),
        V((3, G, W, C), bf16), V((3, G, W, C), bf16),
        V((M, C, T), bf16), V((M, C, T), bf16), V((M, C, T), bf16),
        V((M, C, T), bf16), V((M, C, T), bf16),
        V((8, T), f32), V((n, 8, T), f32), V((8, C), f32), V((F, 8, C), f32),
        V((krows, C), f32), V((krows, C), f32), V((krows, C), f32), V((G, krows, C), f32),
        V((D, 128), f32), V((D, 128), f32),
        S((n,)), S((n,)), S((n,)), S((n,)), S((4,)), S((4,)),
        S((3,)), S((3,)), S((3, G)), S((3, G)),
        S(()), S(()), S((M,)), S((M,)), S((n,)), S((n,)), S((F,)), S((F,)),
        S(()), S(()), S((G,)), S((G,)),
    ]
    out = jax.ShapeDtypeStruct
    vmem = pl.BlockSpec(memory_space=pltpu.VMEM)
    dx, vg, gg, pg, kg, gb = pl.pallas_call(
        functools.partial(kernel, n, F),
        out_shape=[
            out((C, T), bf16), out((W, C), f32), out((W, C), f32), out((W, C), f32),
            out((taps, C), f32), out((8, C), f32),
        ],
        in_specs=[vmem] * 9,
        out_specs=[vmem] * 6,
        scratch_shapes=scratch,
        compiler_params=pltpu.CompilerParams(
            collective_id=0, has_side_effects=True, vmem_limit_bytes=60 * 1024 * 1024
        ),
    )(
        inputs, upstream, norm_gain[None, :], norm_bias[None, :],
        value_weight, gate_weight, conv_kernel, project_weight,
        frame_mask.astype(f32)[None, :],
    )
    return dx, vg.T, gg.T, pg.T, kg, gb[0], gb[1]


def solution(mesh):
    return jax.shard_map(
        functools.partial(on_device, mesh.shape["chan"], mesh.shape["frame"]),
        mesh=mesh,
        in_specs=(
            P("chan", "frame"),
            P(),
            P(),
            P("chan", None),
            P("chan", None),
            P(None, "chan"),
            P("chan", None),
            P("frame"),
            P("chan", "frame"),
        ),
        out_specs=(
            P("chan", "frame"),
            P("chan", "frame"),
            P("chan", "frame"),
            P("chan", "frame"),
            P(None, "chan"),
            P("chan"),
            P("chan"),
        ),
        check_vma=False,
    )
```

```python
import functools

import jax
import jax.numpy as jnp
from jax import lax
from jax.experimental import pallas as pl
from jax.experimental.pallas import tpu as pltpu
from jax.sharding import PartitionSpec as P

eps = 1e-05
pad = 16
row_tile = 64
MESH = pl.DeviceIdType.MESH
f32 = jnp.float32
bf16 = jnp.bfloat16


def dot(a, b, dims):
    return lax.dot_general(a, b, (dims, ((), ())), preferred_element_type=f32)


NN = ((1,), (0,))
NT = ((1,), (1,))


def kernel(
    n, F, x_ref, u_ref, gain_ref, bias_ref, vw_ref, gw_ref, w_ref, pw_ref, keep_ref,
    dx_ref, vg_ref, gg_ref, pg_ref, kg_ref, gb_ref,
    full_x, full_u, normed, vwt, gwt, vp, gs, gl_pad, cg_pad, act_t, conv_t, kacc,
    halo, snd1, rcv1, own1, snd2, rcv2,
    csnd1, crcv1, cown, csnd2, crcv2, st_snd, st_rcv, gb_snd, gb_rcv,
    k_snd, k_rcv1, k_snd2, k_rcv2,
    gain_at, bias_at, sx, rx, su, ru, sh, rh, s1, r1, s2, r2, sc1, rc1, sc2, rc2, sst, rst, sgb, rgb,
    sk1, rk1, sk2, rk2,
):
    C, T = x_ref.shape
    D = vw_ref.shape[1]
    taps = w_ref.shape[0]
    G = F // 2
    M = n // 2
    W = D // F
    me = lax.axis_index("chan")
    fr = lax.axis_index("frame")
    core = lax.rem(me, 2)
    chip = me // 2
    sib = me + 1 - 2 * core
    par = lax.rem(fr, 2)
    grp = fr // 2
    pair = fr + 1 - 2 * par
    pending = []

    def copy(src, dst, ssem, rsem, axis, index):
        return pltpu.make_async_remote_copy(
            src_ref=src, dst_ref=dst, send_sem=ssem, recv_sem=rsem,
            device_id={axis: index}, device_id_type=MESH,
        )

    def send(*args):
        c = copy(*args)
        c.start()
        pending.append(c)

    def rows(i, size):
        return pl.ds(pl.multiple_of(i * size, 16), size)

    barrier = pltpu.get_barrier_semaphore()
    for j in range(1, n):
        pl.semaphore_signal(
            barrier, inc=1, device_id={"chan": lax.rem(me + j, n)}, device_id_type=MESH
        )
    for j in range(1, F):
        pl.semaphore_signal(
            barrier, inc=1, device_id={"frame": lax.rem(fr + j, F)}, device_id_type=MESH
        )
    pl.semaphore_wait(barrier, n - 1 + F - 1)

    for ref, full, ss, rs in ((x_ref, full_x, sx, rx), (u_ref, full_u, su, ru)):
        for j in range(1, M):
            send(ref, full.at[rows(me, C)], ss.at[j], rs.at[me], "chan", lax.rem(me + 2 * j, n))
        send(ref, full.at[rows(me, C)], ss.at[0], rs.at[me], "chan", sib)
    full_x[rows(me, C), :] = x_ref[...]
    full_u[rows(me, C), :] = u_ref[...]
    gain_at[...] = jnp.broadcast_to(gain_ref[...], (128, D)).T
    bias_at[...] = jnp.broadcast_to(bias_ref[...], (128, D)).T
    vwt[...] = vw_ref[...].T
    gwt[...] = gw_ref[...].T

    def arrive(full, ss, rs, src):
        slot = full.at[rows(src, C)]
        copy(slot, slot, ss, rs.at[src], "chan", sib).wait_recv()

    def forward(full, ss, rs):
        for j in range(1, M):
            src = lax.rem(me + 2 * j, n)
            arrive(full, ss.at[0], rs, src)
            slot = full.at[rows(src, C)]
            send(slot, slot, ss.at[M + j - 1], rs.at[src], "chan", sib)

    def rest(full, ss, rs):
        for j in range(M):
            arrive(full, ss.at[0], rs, lax.rem(sib + 2 * j, n))

    forward(full_x, sx, rx)
    rest(full_x, sx, rx)
    total = jnp.zeros((1, T), f32)
    square = jnp.zeros((1, T), f32)
    for j in range(n):
        x = full_x[j * C : (j + 1) * C, :].astype(f32)
        total = total + jnp.sum(x, axis=0, keepdims=True)
        square = square + jnp.sum(x * x, axis=0, keepdims=True)
    mean = total / D
    inv_std = lax.rsqrt(square / D - mean * mean + eps)
    for j in range(n):
        x = full_x[j * C : (j + 1) * C, :].astype(f32)
        normed[j * C : (j + 1) * C, :] = (
            (x - mean) * inv_std * gain_at[j * C : (j + 1) * C, 0:1]
            + bias_at[j * C : (j + 1) * C, 0:1]
        ).astype(bf16)
    keep = keep_ref[...]
    vp[...] = dot(vw_ref[...], normed[...], NN)
    gs[...] = jax.nn.sigmoid(dot(gw_ref[...], normed[...], NN))
    glu = (vp[...] * gs[...] * keep).astype(bf16).astype(f32)
    gl_pad[0, pad : pad + T, :] = glu.T

    def edges(ref, which):
        right, left = lax.rem(fr + 1, F), lax.rem(fr + F - 1, F)
        a, b = 2 * which, 2 * which + 1
        send(ref.at[0, T : T + pad], halo.at[a], sh.at[a], rh.at[a], "frame", right)
        send(ref.at[0, pad : 2 * pad], halo.at[b], sh.at[b], rh.at[b], "frame", left)

    def edges_done(ref, which):
        a, b = 2 * which, 2 * which + 1
        copy(halo.at[a], halo.at[a], sh.at[a], rh.at[a], "frame", pair).wait_recv()
        copy(halo.at[b], halo.at[b], sh.at[b], rh.at[b], "frame", pair).wait_recv()
        ref[0, 0:pad, :] = jnp.where(fr > 0, halo[a], 0.0)
        ref[0, pad + T : T + 2 * pad, :] = jnp.where(fr < F - 1, halo[b], 0.0)
        span = T + 2 * pad - 8
        for p in range(1, 8):
            ref[p, 0:span, :] = ref[0, p : p + span, :]

    edges(gl_pad, 0)
    forward(full_u, su, ru)
    rest(full_u, su, ru)
    act_t[...] = dot(pw_ref[...], full_u[...], NN).astype(bf16).astype(f32).T
    edges_done(gl_pad, 0)

    lane_tile = 128 if C % 128 == 0 else C
    reach = taps // 2
    shift = pad - reach

    def window(ref, start, offset, lanes):
        return ref[offset % 8, pl.ds(start + offset // 8 * 8, row_tile), lanes]

    def conv_rows(i, carry):
        start = pl.multiple_of(i * row_tile, row_tile)
        for c0 in range(0, C, lane_tile):
            lanes = slice(c0, c0 + lane_tile)
            acc = jnp.zeros((row_tile, lane_tile), f32)
            for k in range(taps):
                acc = acc + w_ref[k : k + 1, lanes] * window(gl_pad, start, k + shift, lanes)
            s = jax.nn.sigmoid(acc)
            conv_t[pl.ds(start, row_tile), lanes] = (acc * s).astype(bf16)
            grad = act_t[pl.ds(start, row_tile), lanes] * (s + acc * s * (1.0 - s))
            cg_pad[0, pl.ds(start + pad, row_tile), lanes] = grad.astype(bf16).astype(f32)
        return carry

    lax.fori_loop(0, T // row_tile, conv_rows, 0)
    edges(cg_pad, 1)

    def part(arr, grad_of, fulls):
        for j in range(1, G + 1):
            m = lax.rem(grp + j, G)
            snd1[arr, m] = grad_of(fulls[rows(2 * m + 1 - par, W), :]).astype(bf16)
            send(snd1.at[arr, m], rcv1.at[arr, m], s1.at[arr, j - 1], r1.at[arr, j - 1], "frame", pair)

    def part_arrives(arr, j):
        slot = rcv1.at[arr, lax.rem(grp + j, G)]
        copy(slot, slot, s1.at[arr, j - 1], r1.at[arr, j - 1], "frame", pair).wait_recv()

    def own_part(arr, grad_of, fulls):
        for m in range(G):
            own1[arr, m] = grad_of(fulls[rows(2 * m + par, W), :])

    def project_of(block):
        return dot(block, conv_t[...], NN)

    part(0, project_of, full_u)
    edges_done(cg_pad, 1)
    kacc[...] = jnp.zeros_like(kacc)

    def back_rows(i, carry):
        start = pl.multiple_of(i * row_tile, row_tile)
        for c0 in range(0, C, lane_tile):
            lanes = slice(c0, c0 + lane_tile)
            acc = jnp.zeros((row_tile, lane_tile), f32)
            here = window(cg_pad, start, pad, lanes)
            for k in range(taps):
                acc = acc + w_ref[k : k + 1, lanes] * window(cg_pad, start, pad + reach - k, lanes)
                prod = here * window(gl_pad, start, k + shift, lanes)
                kacc[8 * k : 8 * k + 8, lanes] += jnp.sum(
                    prod.reshape(row_tile // 8, 8, lane_tile), axis=0
                )
            act_t[pl.ds(start, row_tile), lanes] = acc
        return carry

    lax.fori_loop(0, T // row_tile, back_rows, 0)
    glu_grad = act_t[...].T * keep * gs[...]
    value_back = glu_grad.astype(bf16)
    gate_back = (glu_grad * vp[...] * (1.0 - gs[...])).astype(bf16)

    def value_of(block):
        return dot(block, value_back, NT)

    def gate_of(block):
        return dot(block, gate_back, NT)

    part(1, value_of, normed)

    def partial_term(j):
        return (
            dot(vwt[rows(j, C), :], value_back, NN) + dot(gwt[rows(j, C), :], gate_back, NN)
        ).astype(bf16)

    for m in range(M):
        csnd1[m] = partial_term(2 * m + 1 - core)
    send(csnd1, crcv1, sc1, rc1, "chan", sib)
    part(2, gate_of, normed)
    k_snd[...] = jnp.sum(kacc[...].reshape(kacc.shape[0] // 8, 8, C), axis=1)
    send(k_snd, k_rcv1, sk1, rk1, "frame", pair)
    for m in range(M):
        cown[m] = partial_term(2 * m + core)

    def second(arr):
        for j in range(1, G):
            part_arrives(arr, j)
            other = lax.rem(grp + j, G)
            snd2[arr, j] = (own1[arr, other] + rcv1[arr, other].astype(f32)).astype(bf16)
            send(
                snd2.at[arr, j], rcv2.at[arr, j], s2.at[arr, j], r2.at[arr, j],
                "frame", 2 * other + par,
            )

    own_part(0, project_of, full_u)
    second(0)

    copy(csnd1, crcv1, sc1, rc1, "chan", sib).wait_recv()
    for j in range(1, M):
        other = lax.rem(chip + j, M)
        csnd2[j] = (cown[other].astype(f32) + crcv1[other].astype(f32)).astype(bf16)
        send(
            csnd2.at[j], crcv2.at[j], sc2.at[j], rc2.at[j], "chan", 2 * other + core
        )
    own_part(1, value_of, normed)
    own_part(2, gate_of, normed)
    second(1)

    grad = cown[chip].astype(f32) + crcv1[chip].astype(f32)
    for j in range(1, M):
        copy(csnd2.at[j], crcv2.at[j], sc2.at[j], rc2.at[j], "chan", sib).wait_recv()
        grad = grad + crcv2[j].astype(f32)
    vp[...] = grad
    centred = (x_ref[...].astype(f32) - mean) * inv_std
    scaled = grad * gain_at[rows(me, C), 0:1]
    st_snd[0:1, :] = jnp.sum(scaled, axis=0, keepdims=True)
    st_snd[1:2, :] = jnp.sum(scaled * centred, axis=0, keepdims=True)
    st_snd[2:8, :] = jnp.zeros((6, T), f32)
    for j in range(1, n):
        send(st_snd, st_rcv.at[j], sst.at[j], rst.at[j], "chan", lax.rem(me + j, n))
    gain_col = jnp.sum(grad * centred, axis=1, keepdims=True)
    bias_col = jnp.sum(grad, axis=1, keepdims=True)
    lane = lax.broadcasted_iota(jnp.int32, (C, 128), 1)
    gb_snd[...] = jnp.where(lane == 0, gain_col, bias_col).T[0:8, :]
    for j in range(1, F):
        send(gb_snd, gb_rcv.at[j], sgb.at[j], rgb.at[j], "frame", lax.rem(fr + j, F))

    copy(k_snd, k_rcv1, sk1, rk1, "frame", pair).wait_recv()
    k_snd2[...] = k_snd[...] + k_rcv1[...]
    for j in range(1, G):
        send(
            k_snd2, k_rcv2.at[j], sk2.at[j], rk2.at[j], "frame",
            2 * lax.rem(grp + j, G) + par,
        )
    second(2)

    stats = st_snd[...]
    for j in range(1, n):
        copy(st_snd, st_rcv.at[j], sst.at[j], rst.at[j], "chan", sib).wait_recv()
        stats = stats + st_rcv[j]
    stats = stats / D
    centred = (x_ref[...].astype(f32) - mean) * inv_std
    dx_ref[...] = (
        u_ref[...].astype(f32)
        + inv_std * (vp[...] * gain_at[rows(me, C), 0:1] - stats[0:1, :] - centred * stats[1:2, :])
    ).astype(bf16)

    both = gb_snd[...]
    for j in range(1, F):
        copy(gb_snd, gb_rcv.at[j], sgb.at[j], rgb.at[j], "frame", pair).wait_recv()
        both = both + gb_rcv[j]
    gb_ref[...] = both
    taps_sum = k_snd2[...]
    for j in range(1, G):
        copy(k_snd2, k_rcv2.at[j], sk2.at[j], rk2.at[j], "frame", pair).wait_recv()
        taps_sum = taps_sum + k_rcv2[j]
    kg_ref[...] = taps_sum[0:taps, :]

    for arr, out in ((0, pg_ref), (1, vg_ref), (2, gg_ref)):
        part_arrives(arr, G)
        acc = own1[arr, grp] + rcv1[arr, grp].astype(f32)
        for j in range(1, G):
            copy(
                snd2.at[arr, j], rcv2.at[arr, j], s2.at[arr, j], r2.at[arr, j], "frame", pair
            ).wait_recv()
            acc = acc + rcv2[arr, j].astype(f32)
        out[...] = acc

    for c in pending:
        c.wait_send()


def on_device(
    n, F, inputs, norm_gain, norm_bias, value_weight, gate_weight, conv_kernel,
    project_weight, frame_mask, upstream,
):
    C, T = inputs.shape
    D = value_weight.shape[1]
    taps = conv_kernel.shape[0]
    krows = -(-taps // 8) * 8
    G, M, W = F // 2, n // 2, D // F
    V = pltpu.VMEM
    S = pltpu.SemaphoreType.DMA
    scratch = [
        V((D, T), bf16), V((D, T), bf16), V((D, T), bf16), V((D, C), bf16), V((D, C), bf16),
        V((C, T), f32), V((C, T), f32), V((8, T + 2 * pad, C), f32), V((8, T + 2 * pad, C), f32),
        V((T, C), f32), V((T, C), bf16), V((8 * krows, C), f32),
        V((4, pad, C), f32),
        V((3, G, W, C), bf16), V((3, G, W, C), bf16), V((3, G, W, C), f32),
        V((3, G, W, C), bf16), V((3, G, W, C), bf16),
        V((M, C, T), bf16), V((M, C, T), bf16), V((M, C, T), bf16),
        V((M, C, T), bf16), V((M, C, T), bf16),
        V((8, T), f32), V((n, 8, T), f32), V((8, C), f32), V((F, 8, C), f32),
        V((krows, C), f32), V((krows, C), f32), V((krows, C), f32), V((G, krows, C), f32),
        V((D, 128), f32), V((D, 128), f32),
        S((n,)), S((n,)), S((n,)), S((n,)), S((4,)), S((4,)),
        S((3, G)), S((3, G)), S((3, G)), S((3, G)),
        S(()), S(()), S((M,)), S((M,)), S((n,)), S((n,)), S((F,)), S((F,)),
        S(()), S(()), S((G,)), S((G,)),
    ]
    out = jax.ShapeDtypeStruct
    vmem = pl.BlockSpec(memory_space=pltpu.VMEM)
    dx, vg, gg, pg, kg, gb = pl.pallas_call(
        functools.partial(kernel, n, F),
        out_shape=[
            out((C, T), bf16), out((W, C), f32), out((W, C), f32), out((W, C), f32),
            out((taps, C), f32), out((8, C), f32),
        ],
        in_specs=[vmem] * 9,
        out_specs=[vmem] * 6,
        scratch_shapes=scratch,
        compiler_params=pltpu.CompilerParams(
            collective_id=0, has_side_effects=True, vmem_limit_bytes=60 * 1024 * 1024
        ),
    )(
        inputs, upstream, norm_gain[None, :], norm_bias[None, :],
        value_weight, gate_weight, conv_kernel, project_weight,
        frame_mask.astype(f32)[None, :],
    )
    return dx, vg.T, gg.T, pg.T, kg, gb[0], gb[1]


def solution(mesh):
    return jax.shard_map(
        functools.partial(on_device, mesh.shape["chan"], mesh.shape["frame"]),
        mesh=mesh,
        in_specs=(
            P("chan", "frame"),
            P(),
            P(),
            P("chan", None),
            P("chan", None),
            P(None, "chan"),
            P("chan", None),
            P("frame"),
            P("chan", "frame"),
        ),
        out_specs=(
            P("chan", "frame"),
            P("chan", "frame"),
            P("chan", "frame"),
            P("chan", "frame"),
            P(None, "chan"),
            P("chan"),
            P("chan"),
        ),
        check_vma=False,
    )
```
